1024 devices in a mesh: ctx: 64 (over x, y), head: 16 (over z, core).
Axes of the slice: x: 8, y: 8, z: 8, core: 2. Of those that a mesh axis runs over, the one named last changes fastest.
Arguments:
- queries: bfloat16 [12288, 64, 128], P(('ctx', 'head')), may hold values from -36 to 36
- keys: bfloat16 [131072, 16, 128], P('ctx', 'head'), may hold values from -5.5 to 5.5
- values: bfloat16 [131072, 16, 128], P('ctx', 'head'), may hold values from -6 to 6
- out_grad: bfloat16 [12288, 64, 128], P(('ctx', 'head')), may hold values from -192 to 192
- selected: int32 [16, 192, 16], P('head'), may hold values from 0 to 2047, as said below
Outputs:
- query_grad: bfloat16 [12288, 64, 128], P(('ctx', 'head'))
- key_grad: bfloat16 [131072, 16, 128], P('ctx', 'head')
- value_grad: bfloat16 [131072, 16, 128], P('ctx', 'head')
The draws below stay inside these ranges and needn't reach their ends.
Inputs may be any that keep to these rules, and one draw needn't show every extreme that they name: The 16 blocks of one query block and group are distinct, and no block is selected twice by the query blocks of one index of ctx in one group. Key blocks j * 32 to (j + 1) * 32 - 1 are held by index j of ctx; the 3 query blocks of one index of ctx select at most 1 block held by any one index of ctx, for each group, and in each group some index of ctx has exactly 1 of its blocks selected by the query blocks of every index of ctx.
All inputs are finite; a program needn't handle non-finite values.
Results may differ from the reference program's by a relative error of at most 0.0049.
Values may be sent and summed in bfloat16 or wider, within the bound.
No kernel may reach another device: no remote copies, remote signals or barrier semaphores. Data moves between devices by JAX's collectives and lax.ppermute only.
A program may use at most 32 MiB of HBM per device.

```python
import jax
import jax.numpy as jnp
from jax import lax

HEAD_DIM = 128
GROUP_HEADS = 4
BLOCK = 64
SELECTED = 16
KV_GROUPS = 16
HEADS = 64
QUERIES = 12288
CONTEXT = 131072
QUERY_BLOCKS = 3
QBLOCKS_ALL = 192
OWNER_BLOCKS = 32
SLOTS = 1


def selections(key):
    base_key = jax.random.fold_in(key, 11)
    ctx_count = QBLOCKS_ALL // QUERY_BLOCKS
    slot_total = ctx_count * SLOTS
    wanted = QUERY_BLOCKS * SELECTED
    owner_slot = jnp.arange(slot_total, dtype=jnp.int32) // SLOTS
    rank_slot = jnp.arange(slot_total, dtype=jnp.int32) % SLOTS

    def group(group_key):
        key_a, key_b, key_d = jax.random.split(group_key, 3)
        favour = jax.random.randint(key_a, (ctx_count,), 0, 4)
        hottest = jax.random.randint(key_b, (), 0, ctx_count)
        weight = favour[owner_slot] + 4 * (owner_slot == hottest).astype(jnp.int32)

        def requester(one_key):
            key_e, key_f, key_g = jax.random.split(one_key, 3)
            offset = jax.random.randint(key_g, (ctx_count,), 0, OWNER_BLOCKS)
            score_int = weight * slot_total + jax.random.permutation(key_e, slot_total).astype(jnp.int32)
            ignored, picked = lax.top_k(score_int, wanted)
            picked = picked[jax.random.permutation(key_f, wanted)]
            owner_now = owner_slot[picked]
            local_now = (offset[owner_now] + rank_slot[picked]) % OWNER_BLOCKS
            return (owner_now * OWNER_BLOCKS + local_now).reshape(QUERY_BLOCKS, SELECTED)
        return jax.vmap(requester)(jax.random.split(key_d, ctx_count)).reshape(QBLOCKS_ALL, SELECTED)
    return jax.vmap(group)(jax.random.split(base_key, KV_GROUPS)).astype(jnp.int32)


def key_noise(base_key, rows):

    def single(row):
        row_key = jax.random.fold_in(base_key, row)
        noise = jax.random.truncated_normal(row_key, -4.5, 4.5, (KV_GROUPS, HEAD_DIM), jnp.float32)
        return (noise, noise)
    return jax.vmap(single)(rows)


def key_rows(base_key, rows):
    full_rows, raw_noise = key_noise(base_key, rows)
    return full_rows


def draw_keys(key, part):
    rows = jnp.arange(CONTEXT, dtype=jnp.int32)
    return key_rows(jax.random.fold_in(key, 22), rows).astype(jnp.bfloat16)


def draw_selected(key, part):
    return selections(key)


def draw_queries(key, part):
    query_key = jax.random.fold_in(key, 33)
    shape_all = (QUERIES, HEADS, HEAD_DIM)
    return jax.random.truncated_normal(query_key, -4.5, 4.5, shape_all, jnp.float32).astype(jnp.bfloat16)


def shard_levels(key, dims, pieces, low, high):
    level, own = 1.0, jax.random.fold_in(key, 6)
    for dim, parts in pieces:
        draws = jnp.exp(jax.random.uniform(jax.random.fold_in(own, dim), (parts,), jnp.float32, low / len(pieces), high / len(pieces)))
        level = level * jnp.repeat(draws, dims[dim] // parts).reshape([-1 if axis == dim else 1 for axis in range(len(dims))])
    return level


def bell_draw(stream_key, shape, scale, most, cuts=(), kind=jnp.bfloat16):
    drawn = scale * jax.random.normal(stream_key, shape, jnp.float32)
    if cuts:
        drawn = drawn * shard_levels(stream_key, shape, cuts, -0.22, 0.18)
    return jnp.clip(drawn, -most, most).astype(kind)


def setup_inputs(seed: int = 0) -> dict:
    arg_keys = jax.random.split(jax.random.key(seed), 6)
    queries = draw_queries(jax.random.fold_in(arg_keys[5], 71), 0)
    keys = draw_keys(jax.random.fold_in(arg_keys[5], 71), 0)
    values = bell_draw(arg_keys[2], (CONTEXT, KV_GROUPS, HEAD_DIM), 1.0, 6.0, ((0, 64), (1, 16)))
    out_grad = bell_draw(arg_keys[3], (QUERIES, HEADS, HEAD_DIM), 32.0, 192.0, ((0, 1024),))
    selected = draw_selected(jax.random.fold_in(arg_keys[5], 71), 0)
    return {"queries": queries, "keys": keys, "values": values, "out_grad": out_grad, "selected": selected}


def gather_group(table, picks):
    return jax.vmap(lambda plane, chosen: plane[chosen])(table, picks)


def reference(queries, keys, values, out_grad, selected):
    inv_root = HEAD_DIM ** -0.5
    key_table = jnp.transpose(keys.reshape(CONTEXT // BLOCK, BLOCK, KV_GROUPS, HEAD_DIM), (2, 0, 1, 3))
    value_table = jnp.transpose(values.reshape(CONTEXT // BLOCK, BLOCK, KV_GROUPS, HEAD_DIM), (2, 0, 1, 3))
    query_blocks = queries.reshape(QBLOCKS_ALL, BLOCK, KV_GROUPS, GROUP_HEADS, HEAD_DIM)
    grad_blocks = out_grad.reshape(QBLOCKS_ALL, BLOCK, KV_GROUPS, GROUP_HEADS, HEAD_DIM)
    groups = jnp.arange(KV_GROUPS, dtype=jnp.int32)

    def step(carry, index):
        key_acc, value_acc = carry
        picks = lax.dynamic_index_in_dim(selected, index, 1, keepdims=False)
        selected_key_rows = gather_group(key_table, picks).reshape(KV_GROUPS, SELECTED * BLOCK, HEAD_DIM).astype(jnp.float32)
        selected_value_rows = gather_group(value_table, picks).reshape(KV_GROUPS, SELECTED * BLOCK, HEAD_DIM).astype(jnp.float32)
        q_now = lax.dynamic_index_in_dim(query_blocks, index, 0, keepdims=False).astype(jnp.float32)
        g_now = lax.dynamic_index_in_dim(grad_blocks, index, 0, keepdims=False).astype(jnp.float32)
        scores = jnp.einsum("qghd,gkd->ghqk", q_now, selected_key_rows) * inv_root
        row_peak = jnp.max(scores, axis=-1, keepdims=True)
        lifted = jnp.exp(scores - row_peak)
        attend = lifted / jnp.sum(lifted, axis=-1, keepdims=True)
        grad_weights = jnp.einsum("qghd,gkd->ghqk", g_now, selected_value_rows)
        row_delta = jnp.sum(attend * grad_weights, axis=-1, keepdims=True)
        score_gradient = lax.optimization_barrier((attend * (grad_weights - row_delta) * inv_root).astype(jnp.bfloat16))
        half_attention_weights = lax.optimization_barrier(attend.astype(jnp.bfloat16))
        wide_scores = score_gradient.astype(jnp.float32)
        wide_attend = half_attention_weights.astype(jnp.float32)
        query_gradient = jnp.einsum("ghqk,gkd->qghd", wide_scores, selected_key_rows).astype(jnp.bfloat16)
        dkey = jnp.einsum("ghqk,qghd->gkd", wide_scores, q_now).reshape(KV_GROUPS, SELECTED, BLOCK, HEAD_DIM)
        dvalue = jnp.einsum("ghqk,qghd->gkd", wide_attend, g_now).reshape(KV_GROUPS, SELECTED, BLOCK, HEAD_DIM)
        key_acc = key_acc.at[groups[:, None], picks].add(dkey)
        value_acc = value_acc.at[groups[:, None], picks].add(dvalue)
        return (key_acc, value_acc), query_gradient

    zeros_acc = jnp.zeros((KV_GROUPS, CONTEXT // BLOCK, BLOCK, HEAD_DIM), jnp.float32)
    (key_acc, value_acc), dq_all = lax.scan(step, (zeros_acc, zeros_acc), jnp.arange(QBLOCKS_ALL, dtype=jnp.int32))
    query_grad = dq_all.reshape(QUERIES, HEADS, HEAD_DIM)
    key_grad = jnp.transpose(key_acc, (1, 2, 0, 3)).reshape(CONTEXT, KV_GROUPS, HEAD_DIM).astype(jnp.bfloat16)
    value_grad = jnp.transpose(value_acc, (1, 2, 0, 3)).reshape(CONTEXT, KV_GROUPS, HEAD_DIM).astype(jnp.bfloat16)
    return (query_grad, key_grad, value_grad)
```

```python
import functools

import jax
import jax.numpy as jnp
from jax import lax
from jax.experimental import pallas as pl
from jax.experimental.pallas import tpu as pltpu
from jax.sharding import PartitionSpec as P

BLOCK = 64
SELECTED = 16
CTX = 64
OWNED = 32
QBLOCKS = 3
HEAD_DIM = 128
GROUP_HEADS = 4
ROWS = BLOCK * GROUP_HEADS
PART = 16
SCALE = HEAD_DIM**-0.5
LOG2E = 1.4426950408889634
VMEM_LIMIT = 40 * 1024 * 1024


def wanted_row(rows, index):
    first = rows[QBLOCKS * index]
    return jnp.maximum(jnp.maximum(first, rows[QBLOCKS * index + 1]), rows[QBLOCKS * index + 2])


def pack_kernel(rows, keys, values, packed):
    base = pl.program_id(0) * PART

    def copy(index, carry):
        row = jnp.maximum(wanted_row(rows, base + index), 0)
        packed[index, 0] = keys[row]
        packed[index, 1] = values[row]
        return carry

    lax.fori_loop(0, PART, copy, 0, unroll=4)


def pack(rows, keys, values):
    whole = pl.BlockSpec((OWNED, BLOCK, HEAD_DIM), lambda i, rows: (0, 0, 0))
    return pl.pallas_call(
        pack_kernel,
        out_shape=jax.ShapeDtypeStruct((CTX, 2, BLOCK, HEAD_DIM), jnp.bfloat16),
        grid_spec=pltpu.PrefetchScalarGridSpec(
            num_scalar_prefetch=1,
            grid=(CTX // PART,),
            in_specs=[whole, whole],
            out_specs=pl.BlockSpec((PART, 2, BLOCK, HEAD_DIM), lambda i, rows: (i, 0, 0, 0)),
        ),
        compiler_params=pltpu.CompilerParams(vmem_limit_bytes=VMEM_LIMIT),
        name="pack_blocks",
    )(rows, keys, values)


def attend_kernel(slots, fetched, queries, grads, query_grad, terms, key_rows, value_rows):
    step = pl.program_id(0)

    @pl.when(step == 0)
    def _():
        terms[...] = jnp.zeros_like(terms)

    for s in range(SELECTED):
        slot = slots[s, step]
        key_rows[pl.ds(s * BLOCK, BLOCK), :] = fetched[slot, 0]
        value_rows[pl.ds(s * BLOCK, BLOCK), :] = fetched[slot, 1]
    q_now = queries[...]
    g_now = grads[...]
    rows_last = (((1,), (1,)), ((), ()))
    rows_first = (((0,), (0,)), ((), ()))
    scores = lax.dot_general(key_rows[...], q_now, rows_last, preferred_element_type=jnp.float32)
    peak = jnp.max(scores, axis=0, keepdims=True)
    lifted = jnp.exp2((scores - peak) * (SCALE * LOG2E))
    inverse = 1.0 / jnp.sum(lifted, axis=0, keepdims=True)
    attend = lifted * inverse
    weights = lax.dot_general(value_rows[...], g_now, rows_last, preferred_element_type=jnp.float32)
    delta = jnp.sum(attend * weights, axis=0, keepdims=True)
    score_grad = (attend * (weights - delta) * SCALE).astype(jnp.bfloat16)
    half = attend.astype(jnp.bfloat16)
    flipped = lax.dot_general(key_rows[...], score_grad, rows_first, preferred_element_type=jnp.float32)
    query_grad[...] = flipped.T.astype(jnp.bfloat16)
    key_terms = jnp.dot(score_grad, q_now, preferred_element_type=jnp.float32).astype(jnp.bfloat16)
    value_terms = jnp.dot(half, g_now, preferred_element_type=jnp.float32).astype(jnp.bfloat16)
    for s in range(SELECTED):
        slot = slots[s, step]
        terms[slot, 0] = key_terms[s * BLOCK : (s + 1) * BLOCK]
        terms[slot, 1] = value_terms[s * BLOCK : (s + 1) * BLOCK]


def attend_backward(slots, fetched, queries, grads):
    whole = pl.BlockSpec((CTX, 2, BLOCK, HEAD_DIM), lambda i, slots: (0, 0, 0, 0))
    part = pl.BlockSpec((ROWS, HEAD_DIM), lambda i, slots: (i, 0))
    return pl.pallas_call(
        attend_kernel,
        out_shape=(
            jax.ShapeDtypeStruct((QBLOCKS * ROWS, HEAD_DIM), jnp.bfloat16),
            jax.ShapeDtypeStruct((CTX, 2, BLOCK, HEAD_DIM), jnp.bfloat16),
        ),
        grid_spec=pltpu.PrefetchScalarGridSpec(
            num_scalar_prefetch=1,
            grid=(QBLOCKS,),
            in_specs=[whole, part, part],
            out_specs=(part, whole),
            scratch_shapes=[
                pltpu.VMEM((SELECTED * BLOCK, HEAD_DIM), jnp.bfloat16),
                pltpu.VMEM((SELECTED * BLOCK, HEAD_DIM), jnp.bfloat16),
            ],
        ),
        compiler_params=pltpu.CompilerParams(vmem_limit_bytes=VMEM_LIMIT),
        name="attend_backward",
    )(slots, fetched, queries, grads)


def sum_kernel(rows, terms, key_grad, value_grad, key_sum, value_sum):
    step = pl.program_id(0)

    @pl.when(step == 0)
    def _():
        key_sum[...] = jnp.zeros_like(key_sum)
        value_sum[...] = jnp.zeros_like(value_sum)

    def add(index, carry):
        row = wanted_row(rows, step * PART + index)

        @pl.when(row >= 0)
        def _():
            key_sum[row] += terms[index, 0].astype(jnp.float32)
            value_sum[row] += terms[index, 1].astype(jnp.float32)

        return carry

    lax.fori_loop(0, PART, add, 0)

    @pl.when(step == pl.num_programs(0) - 1)
    def _():
        key_grad[...] = key_sum[...].astype(jnp.bfloat16)
        value_grad[...] = value_sum[...].astype(jnp.bfloat16)


def owner_sum(rows, terms):
    whole = pl.BlockSpec((OWNED, BLOCK, HEAD_DIM), lambda i, rows: (0, 0, 0))
    grad = jax.ShapeDtypeStruct((OWNED, BLOCK, HEAD_DIM), jnp.bfloat16)
    return pl.pallas_call(
        sum_kernel,
        out_shape=(grad, grad),
        grid_spec=pltpu.PrefetchScalarGridSpec(
            num_scalar_prefetch=1,
            grid=(CTX // PART,),
            in_specs=[pl.BlockSpec((PART, 2, BLOCK, HEAD_DIM), lambda i, rows: (i, 0, 0, 0))],
            out_specs=(whole, whole),
            scratch_shapes=[
                pltpu.VMEM((OWNED, BLOCK, HEAD_DIM), jnp.float32),
                pltpu.VMEM((OWNED, BLOCK, HEAD_DIM), jnp.float32),
            ],
        ),
        compiler_params=pltpu.CompilerParams(vmem_limit_bytes=VMEM_LIMIT),
        name="owner_sum",
    )(rows, terms)


def exchange(blocks):
    return lax.all_to_all(blocks, "ctx", split_axis=0, concat_axis=0, tiled=True)


def my_heads(tokens, head):
    gathered = lax.all_gather(tokens, "head", axis=0, tiled=True)
    mine = lax.dynamic_slice_in_dim(gathered, head * GROUP_HEADS, GROUP_HEADS, 1)
    return mine.reshape(QBLOCKS * ROWS, HEAD_DIM)


def per_device(queries, keys, values, out_grad, selected):
    ctx, head = lax.axis_index("ctx"), lax.axis_index("head")
    table = selected[0].T
    rows = jnp.max(jnp.where(table // OWNED == ctx, table % OWNED, -1), axis=0)
    slots = lax.dynamic_slice_in_dim(table, ctx * QBLOCKS, QBLOCKS, 1) // OWNED
    blocks = (OWNED, BLOCK, HEAD_DIM)
    packed = pack(rows, keys.reshape(blocks), values.reshape(blocks))
    fetched = exchange(packed)
    query_grad, terms = attend_backward(slots, fetched, my_heads(queries, head), my_heads(out_grad, head))
    back = exchange(terms)
    tokens = queries.shape[0]
    gathered = lax.all_gather(query_grad, "head", axis=0)
    mine = lax.dynamic_slice_in_dim(gathered, head * tokens * GROUP_HEADS, tokens * GROUP_HEADS, 1)
    mine = mine.reshape(gathered.shape[0], tokens, GROUP_HEADS, HEAD_DIM)
    query_grad = mine.transpose(1, 0, 2, 3).reshape(queries.shape)
    key_grad, value_grad = owner_sum(rows, back)
    return query_grad, key_grad.reshape(keys.shape), value_grad.reshape(values.shape)


def solution(mesh):
    tokens = P(("ctx", "head"), None, None)
    context = P("ctx", "head", None)
    return jax.shard_map(
        per_device,
        mesh=mesh,
        in_specs=(tokens, context, context, tokens, P("head", None, None)),
        out_specs=(tokens, context, context),
        check_vma=False,
    )
```

```python
import functools

import jax
import jax.numpy as jnp
from jax import lax
from jax.experimental import pallas as pl
from jax.experimental.pallas import tpu as pltpu
from jax.sharding import PartitionSpec as P

BLOCK = 64
SELECTED = 16
CTX = 64
OWNED = 32
QBLOCKS = 3
QBLOCKS_ALL = 192
HEAD_DIM = 128
GROUP_HEADS = 4
ROWS = BLOCK * GROUP_HEADS
KEYS = SELECTED * BLOCK
TOKENS = 12
PIECE = TOKENS * GROUP_HEADS
PLANES = 8
CORES = 2
SCALE = HEAD_DIM**-0.5
LOG2E = 1.4426950408889634
VMEM_LIMIT = 40 * 1024 * 1024
VMEM_ALL = 62 * 1024 * 1024
VMEM_ATTEND = 52 * 1024 * 1024
BF16 = jnp.bfloat16
F32 = jnp.float32
IN_VMEM = pl.BlockSpec(memory_space=pltpu.VMEM)
IN_SMEM = pl.BlockSpec(memory_space=pltpu.SMEM)
IN_HBM = pl.BlockSpec(memory_space=pltpu.HBM)


def array(*shape, dtype=BF16):
    return jax.ShapeDtypeStruct(shape, dtype)


def wanted_row(rows, index):
    first = rows[0, QBLOCKS * index]
    return jnp.maximum(jnp.maximum(first, rows[0, QBLOCKS * index + 1]), rows[0, QBLOCKS * index + 2])


def pack_kernel(place, table, keys, values, packed, rows, key_buf, value_buf, out_buf, row_buf, in_sems, out_sems):
    loads = [
        pltpu.make_async_copy(keys, key_buf, in_sems.at[0]),
        pltpu.make_async_copy(values, value_buf, in_sems.at[1]),
    ]
    for load in loads:
        load.start()
    picks = table[...]
    mine = jnp.where(picks // OWNED == place[0], picks % OWNED, -1)
    row_buf[...] = jnp.max(mine, axis=0, keepdims=True)
    to_scalars = pltpu.make_async_copy(row_buf, rows, in_sems.at[2])
    to_scalars.start()
    to_scalars.wait()
    for load in loads:
        load.wait()
    parts = out_sems.shape[0]
    size = CTX // parts

    def store(part):
        span = pl.ds(part * size, size)
        return pltpu.make_async_copy(out_buf.at[span], packed.at[span], out_sems.at[part])

    for part in range(parts):

        def copy(index, carry):
            row = jnp.maximum(wanted_row(rows, index), 0)
            out_buf[index, 0] = key_buf[row]
            out_buf[index, 1] = value_buf[row]
            return carry

        lax.fori_loop(part * size, (part + 1) * size, copy, 0, unroll=4)
        store(part).start()
    for part in range(parts):
        store(part).wait()


def pack(place, table, keys, values):
    return pl.pallas_call(
        pack_kernel,
        out_shape=(array(CTX, 2, BLOCK, HEAD_DIM), array(1, QBLOCKS_ALL, dtype=jnp.int32)),
        in_specs=[IN_SMEM, IN_VMEM, IN_HBM, IN_HBM],
        out_specs=(IN_HBM, IN_SMEM),
        scratch_shapes=[
            pltpu.VMEM((OWNED, BLOCK, HEAD_DIM), BF16),
            pltpu.VMEM((OWNED, BLOCK, HEAD_DIM), BF16),
            pltpu.VMEM((CTX, 2, BLOCK, HEAD_DIM), BF16),
            pltpu.VMEM((1, QBLOCKS_ALL), jnp.int32),
            pltpu.SemaphoreType.DMA((3,)),
            pltpu.SemaphoreType.DMA((4,)),
        ],
        compiler_params=pltpu.CompilerParams(vmem_limit_bytes=VMEM_ALL),
        name="pack_blocks",
    )(place, table, keys, values)


def halves(first, second):
    low = lax.broadcasted_iota(jnp.int32, first.shape, first.ndim - 2) < GROUP_HEADS
    axis = first.ndim - 2
    return (
        jnp.where(low, first, pltpu.roll(second, GROUP_HEADS, axis)),
        jnp.where(low, pltpu.roll(first, GROUP_HEADS, axis), second),
    )


def split_kernel(place, rows, queries, grads, keep, send):
    plane, core = place[1], place[2]
    for kind, ref in enumerate((queries, grads)):
        tokens = ref[...].astype(F32).reshape(TOKENS // 2, 2, PLANES, 8, HEAD_DIM)
        low, high = halves(tokens[:, 0], tokens[:, 1])
        mine = jnp.where(core == 0, low, high).astype(BF16)
        other = jnp.where(core == 0, high, low).astype(BF16)
        for target in range(PLANES):
            shift = (target - plane + PLANES) % PLANES
            keep[shift, kind] = mine[:, target].reshape(PIECE, HEAD_DIM)
            send[shift, kind] = other[:, target].reshape(PIECE, HEAD_DIM)


def split(place, rows, queries, grads):
    out = array(PLANES, 2, PIECE, HEAD_DIM)
    return pl.pallas_call(
        split_kernel,
        out_shape=(out, out),
        in_specs=[IN_SMEM, IN_SMEM, IN_VMEM, IN_VMEM],
        out_specs=(IN_VMEM, IN_VMEM),
        compiler_params=pltpu.CompilerParams(vmem_limit_bytes=VMEM_LIMIT),
        name="split_heads",
    )(place, rows, queries, grads)


def join_kernel(keep, got, *parcels):
    for shift, parcel in enumerate(parcels):
        parcel[0:2] = keep[shift]
        parcel[2:4] = got[shift]


def join(keep, got):
    return pl.pallas_call(
        join_kernel,
        out_shape=(array(4, PIECE, HEAD_DIM),) * PLANES,
        in_specs=[IN_VMEM, IN_VMEM],
        out_specs=(IN_VMEM,) * PLANES,
        compiler_params=pltpu.CompilerParams(vmem_limit_bytes=VMEM_LIMIT),
        name="join_parcels",
    )(keep, got)


def attend_kernel(place, slots, fetched, *refs):
    parcels, terms, results = refs[:PLANES], refs[PLANES], refs[PLANES + 1 : 2 * PLANES + 1]
    q_rows, g_rows, key_rows, value_rows, grad_rows, stage, sems, key_sems, value_sems = refs[2 * PLANES + 1 :]
    plane, core = place[1], place[2]

    def load(step, carry):
        for s in range(SELECTED):
            slot = slots[s, step]
            span = pl.ds(pl.multiple_of(step * KEYS + s * BLOCK, BLOCK), BLOCK)
            pltpu.make_async_copy(fetched.at[slot, 0], key_rows.at[span], key_sems.at[step]).start()
            pltpu.make_async_copy(fetched.at[slot, 1], value_rows.at[span], value_sems.at[step]).start()
        return carry

    lax.fori_loop(0, QBLOCKS, load, 0)
    for shift, parcel in enumerate(parcels):
        source = (plane - shift + PLANES) % PLANES
        for piece, owner in ((0, core), (2, 1 - core)):
            span = pl.ds(pl.multiple_of((source * CORES + owner) * PIECE, 16), PIECE)
            q_rows[span, :] = parcel[piece]
            g_rows[span, :] = parcel[piece + 1]
    rows_last = (((1,), (1,)), ((), ()))
    rows_first = (((0,), (0,)), ((), ()))

    def store(step, s):
        item = step * SELECTED + s
        return pltpu.make_async_copy(stage.at[item], terms.at[slots[s, step]], sems.at[item])

    def block(step, carry):
        chosen = pl.ds(pl.multiple_of(step * KEYS, KEYS), KEYS)
        for rows, load_sems in ((key_rows, key_sems), (value_rows, value_sems)):
            pltpu.make_async_copy(rows.at[chosen], rows.at[chosen], load_sems.at[step]).wait()
        k_now, v_now = key_rows[chosen, :], value_rows[chosen, :]
        span = pl.ds(pl.multiple_of(step * ROWS, ROWS), ROWS)
        q_now = q_rows[span, :]
        g_now = g_rows[span, :]
        scores = lax.dot_general(k_now, q_now, rows_last, preferred_element_type=F32)
        peak = jnp.max(scores, axis=0, keepdims=True)
        lifted = jnp.exp2((scores - peak) * (SCALE * LOG2E))
        inverse = 1.0 / jnp.sum(lifted, axis=0, keepdims=True)
        attend = lifted * inverse
        weights = lax.dot_general(v_now, g_now, rows_last, preferred_element_type=F32)
        delta = jnp.sum(attend * weights, axis=0, keepdims=True)
        score_grad = (attend * (weights - delta) * SCALE).astype(BF16)
        half = attend.astype(BF16)
        flipped = lax.dot_general(k_now, score_grad, rows_first, preferred_element_type=F32)
        grad_rows[span, :] = flipped.T.astype(BF16)
        key_terms = jnp.dot(score_grad, q_now, preferred_element_type=F32).astype(BF16)
        value_terms = jnp.dot(half, g_now, preferred_element_type=F32).astype(BF16)
        for s in range(SELECTED):
            item = step * SELECTED + s
            stage[item, 0] = key_terms[s * BLOCK : (s + 1) * BLOCK]
            stage[item, 1] = value_terms[s * BLOCK : (s + 1) * BLOCK]
            store(step, s).start()
        return carry

    lax.fori_loop(0, QBLOCKS, block, 0)
    for shift, result in enumerate(results):
        target = (plane + shift) % PLANES
        for owner in range(CORES):
            span = pl.ds(pl.multiple_of((target * CORES + owner) * PIECE, 16), PIECE)
            result[owner] = grad_rows[span, :]

    def finish(step, carry):
        for s in range(SELECTED):
            store(step, s).wait()
        return carry

    lax.fori_loop(0, QBLOCKS, finish, 0)


def attend_backward(place, slots, fetched, parcels):
    rows = pltpu.VMEM((QBLOCKS * ROWS, HEAD_DIM), BF16)
    return pl.pallas_call(
        attend_kernel,
        out_shape=(array(CTX, 2, BLOCK, HEAD_DIM),) + (array(CORES, PIECE, HEAD_DIM),) * PLANES,
        in_specs=[IN_SMEM, IN_SMEM, IN_HBM] + [IN_VMEM] * PLANES,
        out_specs=(IN_HBM,) + (IN_VMEM,) * PLANES,
        scratch_shapes=[
            rows,
            rows,
            pltpu.VMEM((QBLOCKS * KEYS, HEAD_DIM), BF16),
            pltpu.VMEM((QBLOCKS * KEYS, HEAD_DIM), BF16),
            rows,
            pltpu.VMEM((QBLOCKS * SELECTED, 2, BLOCK, HEAD_DIM), BF16),
            pltpu.SemaphoreType.DMA((QBLOCKS * SELECTED,)),
            pltpu.SemaphoreType.DMA((QBLOCKS,)),
            pltpu.SemaphoreType.DMA((QBLOCKS,)),
        ],
        compiler_params=pltpu.CompilerParams(vmem_limit_bytes=VMEM_ATTEND),
        name="attend_backward",
    )(place, slots, fetched, *parcels)


def swap_kernel(place, *refs):
    parcels, (keep, send) = refs[:PLANES], refs[PLANES:]
    core = place[2]
    for shift, parcel in enumerate(parcels):
        keep[shift] = parcel[core]
        send[shift] = parcel[1 - core]


def swap(place, parcels):
    out = array(PLANES, PIECE, HEAD_DIM)
    return pl.pallas_call(
        swap_kernel,
        out_shape=(out, out),
        in_specs=[IN_SMEM] + [IN_VMEM] * PLANES,
        out_specs=(IN_VMEM, IN_VMEM),
        compiler_params=pltpu.CompilerParams(vmem_limit_bytes=VMEM_LIMIT),
        name="swap_cores",
    )(place, *parcels)


def merge_kernel(place, keep, got, query_grad):
    plane, core = place[1], place[2]
    shape = (TOKENS // 2, 8, HEAD_DIM)
    even, odd = [], []
    for source in range(PLANES):
        shift = (plane - source + PLANES) % PLANES
        mine = keep[shift].astype(F32).reshape(shape)
        other = got[shift].astype(F32).reshape(shape)
        pair = halves(jnp.where(core == 0, mine, other), jnp.where(core == 0, other, mine))
        even.append(pair[0])
        odd.append(pair[1])
    both = jnp.stack([jnp.stack(even, 1), jnp.stack(odd, 1)], 1)
    query_grad[...] = both.reshape(TOKENS, PLANES * 8, HEAD_DIM).astype(BF16)


def merge(place, keep, got):
    return pl.pallas_call(
        merge_kernel,
        out_shape=array(TOKENS, PLANES * 8, HEAD_DIM),
        in_specs=[IN_SMEM, IN_VMEM, IN_VMEM],
        out_specs=IN_VMEM,
        compiler_params=pltpu.CompilerParams(vmem_limit_bytes=VMEM_LIMIT),
        name="merge_heads",
    )(place, keep, got)


def sum_kernel(rows, terms, key_grad, value_grad, key_sum, value_sum):
    key_sum[...] = jnp.zeros_like(key_sum)
    value_sum[...] = jnp.zeros_like(value_sum)

    def add(index, carry):
        row = wanted_row(rows, index)

        @pl.when(row >= 0)
        def _():
            key_sum[row] += terms[index, 0].astype(F32)
            value_sum[row] += terms[index, 1].astype(F32)

        return carry

    lax.fori_loop(0, CTX, add, 0)
    key_grad[...] = key_sum[...].astype(BF16)
    value_grad[...] = value_sum[...].astype(BF16)


def owner_sum(rows, terms):
    grad = array(OWNED, BLOCK, HEAD_DIM)
    return pl.pallas_call(
        sum_kernel,
        out_shape=(grad, grad),
        in_specs=[IN_SMEM, IN_VMEM],
        out_specs=(IN_VMEM, IN_VMEM),
        scratch_shapes=[pltpu.VMEM((OWNED, BLOCK, HEAD_DIM), F32)] * 2,
        compiler_params=pltpu.CompilerParams(vmem_limit_bytes=VMEM_LIMIT),
        name="owner_sum",
    )(rows, terms)


def exchange(blocks):
    return lax.all_to_all(blocks, "ctx", split_axis=0, concat_axis=0, tiled=True)


def swap_partner(array):
    return lax.ppermute(array, "head", [(i, i ^ 1) for i in range(PLANES * CORES)])


def along_planes(parcels):
    moved = [parcels[0]]
    for shift in range(1, PLANES):
        pairs = [(i, (i + shift * CORES) % (PLANES * CORES)) for i in range(PLANES * CORES)]
        moved.append(lax.ppermute(parcels[shift], "head", pairs))
    return moved


def per_device(queries, keys, values, out_grad, selected):
    ctx, head = lax.axis_index("ctx"), lax.axis_index("head")
    place = jnp.stack([ctx, head >> 1, head & 1]).astype(jnp.int32)
    table = selected[0].T
    slots = lax.dynamic_slice_in_dim(table, ctx * QBLOCKS, QBLOCKS, 1) // OWNED
    blocks = (OWNED, BLOCK, HEAD_DIM)
    packed, rows = pack(place, table, keys.reshape(blocks), values.reshape(blocks))
    fetched = exchange(packed)
    keep, send = split(place, rows, queries, out_grad)
    parcels = along_planes(join(keep, swap_partner(send)))
    terms, *results = attend_backward(place, slots, fetched, parcels)
    back = exchange(terms)
    keep, send = swap(place, along_planes(results))
    query_grad = merge(place, keep, swap_partner(send))
    key_grad, value_grad = owner_sum(rows, back)
    return query_grad, key_grad.reshape(keys.shape), value_grad.reshape(values.shape)


def solution(mesh):
    tokens = P(("ctx", "head"), None, None)
    context = P("ctx", "head", None)
    return jax.shard_map(
        per_device,
        mesh=mesh,
        in_specs=(tokens, context, context, tokens, P("head", None, None)),
        out_specs=(tokens, context, context),
        check_vma=False,
    )
```

```python
import functools

import jax
import jax.numpy as jnp
from jax import lax
from jax.experimental import pallas as pl
from jax.experimental.pallas import tpu as pltpu
from jax.sharding import PartitionSpec as P

BLOCK = 64
SELECTED = 16
CTX = 64
OWNED = 32
QBLOCKS = 3
QBLOCKS_ALL = 192
HEAD_DIM = 128
GROUP_HEADS = 4
ROWS = BLOCK * GROUP_HEADS
KEYS = SELECTED * BLOCK
TOKENS = 12
PIECE = TOKENS * GROUP_HEADS
PLANES = 8
CHUNK = 256
CORES = 2
SCALE = HEAD_DIM**-0.5
LOG2E = 1.4426950408889634
VMEM_LIMIT = 40 * 1024 * 1024
VMEM_ALL = 62 * 1024 * 1024
VMEM_ATTEND = 44 * 1024 * 1024
BF16 = jnp.bfloat16
F32 = jnp.float32
IN_VMEM = pl.BlockSpec(memory_space=pltpu.VMEM)
IN_SMEM = pl.BlockSpec(memory_space=pltpu.SMEM)
IN_HBM = pl.BlockSpec(memory_space=pltpu.HBM)


def array(*shape, dtype=BF16):
    return jax.ShapeDtypeStruct(shape, dtype)


def wanted_row(rows, index):
    first = rows[0, QBLOCKS * index]
    return jnp.maximum(jnp.maximum(first, rows[0, QBLOCKS * index + 1]), rows[0, QBLOCKS * index + 2])


def pack_kernel(table, keys, values, packed, rows, key_buf, value_buf, out_buf, table_buf, row_buf, in_sems, out_sems):
    picked = pltpu.make_async_copy(table, table_buf, in_sems.at[0])
    loads = [
        pltpu.make_async_copy(keys, key_buf, in_sems.at[1]),
        pltpu.make_async_copy(values, value_buf, in_sems.at[2]),
    ]
    picked.start()
    for load in loads:
        load.start()
    picked.wait()
    picks = table_buf[...]
    mine = jnp.where(picks // OWNED == lax.axis_index("ctx"), picks % OWNED, -1)
    row_buf[...] = jnp.max(mine, axis=0, keepdims=True)
    to_scalars = pltpu.make_async_copy(row_buf, rows, in_sems.at[3])
    to_scalars.start()
    to_scalars.wait()
    for load in loads:
        load.wait()
    parts = out_sems.shape[0]
    size = CTX // parts

    def store(part):
        span = pl.ds(part * size, size)
        return pltpu.make_async_copy(out_buf.at[span], packed.at[span], out_sems.at[part])

    for part in range(parts):

        def copy(index, carry):
            row = jnp.maximum(wanted_row(rows, index), 0)
            out_buf[index, 0] = key_buf[row]
            out_buf[index, 1] = value_buf[row]
            return carry

        lax.fori_loop(part * size, (part + 1) * size, copy, 0, unroll=4)
        store(part).start()
    for part in range(parts):
        store(part).wait()


def pack(table, keys, values):
    return pl.pallas_call(
        pack_kernel,
        out_shape=(array(CTX, 2, BLOCK, HEAD_DIM), array(1, QBLOCKS_ALL, dtype=jnp.int32)),
        in_specs=[IN_HBM, IN_HBM, IN_HBM],
        out_specs=(IN_HBM, IN_SMEM),
        scratch_shapes=[
            pltpu.VMEM((OWNED, BLOCK, HEAD_DIM), BF16),
            pltpu.VMEM((OWNED, BLOCK, HEAD_DIM), BF16),
            pltpu.VMEM((CTX, 2, BLOCK, HEAD_DIM), BF16),
            pltpu.VMEM((SELECTED, QBLOCKS_ALL), jnp.int32),
            pltpu.VMEM((1, QBLOCKS_ALL), jnp.int32),
            pltpu.SemaphoreType.DMA((4,)),
            pltpu.SemaphoreType.DMA((8,)),
        ],
        compiler_params=pltpu.CompilerParams(vmem_limit_bytes=VMEM_ALL),
        name="pack_blocks",
    )(table, keys, values)


def halves(first, second):
    low = lax.broadcasted_iota(jnp.int32, first.shape, first.ndim - 2) < GROUP_HEADS
    axis = first.ndim - 2
    return (
        jnp.where(low, first, pltpu.roll(second, GROUP_HEADS, axis)),
        jnp.where(low, pltpu.roll(first, GROUP_HEADS, axis), second),
    )


def split_kernel(rows, queries, grads, keep, send):
    head = lax.axis_index("head")
    plane, core = head // CORES, head % CORES
    for kind, ref in enumerate((queries, grads)):
        tokens = ref[...].astype(F32).reshape(TOKENS // 2, 2, PLANES, 8, HEAD_DIM)
        low, high = halves(tokens[:, 0], tokens[:, 1])
        mine = jnp.where(core == 0, low, high).astype(BF16)
        other = jnp.where(core == 0, high, low).astype(BF16)
        for target in range(PLANES):
            shift = (target - plane + PLANES) % PLANES
            keep[shift, kind] = mine[:, target].reshape(PIECE, HEAD_DIM)
            send[shift, kind] = other[:, target].reshape(PIECE, HEAD_DIM)


def split(rows, queries, grads):
    out = array(PLANES, 2, PIECE, HEAD_DIM)
    return pl.pallas_call(
        split_kernel,
        out_shape=(out, out),
        in_specs=[IN_SMEM, IN_VMEM, IN_VMEM],
        out_specs=(IN_VMEM, IN_VMEM),
        compiler_params=pltpu.CompilerParams(vmem_limit_bytes=VMEM_LIMIT),
        name="split_heads",
    )(rows, queries, grads)


def join_kernel(keep, got, *parcels):
    for shift, parcel in enumerate(parcels):
        parcel[0:2] = keep[shift]
        parcel[2:4] = got[shift]


def join(keep, got):
    return pl.pallas_call(
        join_kernel,
        out_shape=(array(4, PIECE, HEAD_DIM),) * PLANES,
        in_specs=[IN_VMEM, IN_VMEM],
        out_specs=(IN_VMEM,) * PLANES,
        compiler_params=pltpu.CompilerParams(vmem_limit_bytes=VMEM_LIMIT),
        name="join_parcels",
    )(keep, got)


def attend_kernel(slots, unused, fetched, *refs):
    parcels, terms, results = refs[:PLANES], refs[PLANES], refs[PLANES + 1 : 2 * PLANES + 1]
    q_rows, g_rows, key_rows, value_rows, grad_rows, score_buf, weight_buf, delta_buf, stage, sems = refs[2 * PLANES + 1 :]
    head = lax.axis_index("head")
    plane, core = head // CORES, head % CORES
    for shift, parcel in enumerate(parcels):
        source = (plane - shift + PLANES) % PLANES
        for piece, owner in ((0, core), (2, 1 - core)):
            span = pl.ds(pl.multiple_of((source * CORES + owner) * PIECE, 16), PIECE)
            q_rows[span, :] = parcel[piece]
            g_rows[span, :] = parcel[piece + 1]
    rows_last = (((1,), (1,)), ((), ()))
    rows_first = (((0,), (0,)), ((), ()))
    chunks = [pl.ds(start, CHUNK) for start in range(0, KEYS, CHUNK)]
    per_chunk = CHUNK // BLOCK

    def fold(values, reduce):
        return reduce(values.reshape(CHUNK // 8, 8, ROWS), axis=0)

    def store(step, s):
        item = step * SELECTED + s
        return pltpu.make_async_copy(stage.at[item], terms.at[slots[s, step]], sems.at[item])

    def block(step, carry):
        for s in range(SELECTED):
            slot = slots[s, step]
            key_rows[pl.ds(s * BLOCK, BLOCK), :] = fetched[slot, 0]
            value_rows[pl.ds(s * BLOCK, BLOCK), :] = fetched[slot, 1]
        span = pl.ds(pl.multiple_of(step * ROWS, ROWS), ROWS)
        q_now = q_rows[span, :]
        g_now = g_rows[span, :]
        peak = jnp.full((8, ROWS), -jnp.inf, F32)
        for chunk in chunks:
            scores = lax.dot_general(key_rows[chunk, :], q_now, rows_last, preferred_element_type=F32)
            score_buf[chunk, :] = scores
            peak = jnp.maximum(peak, fold(scores, jnp.max))
        peak = jnp.max(peak, axis=0, keepdims=True)
        total = jnp.zeros((8, ROWS), F32)
        delta = jnp.zeros((8, ROWS), F32)
        for chunk in chunks:
            weights = lax.dot_general(value_rows[chunk, :], g_now, rows_last, preferred_element_type=F32)
            lifted = jnp.exp2((score_buf[chunk, :] - peak) * (SCALE * LOG2E))
            score_buf[chunk, :] = lifted
            weight_buf[chunk, :] = weights
            total += fold(lifted, jnp.sum)
            delta += fold(lifted * weights, jnp.sum)
        inverse = 1.0 / jnp.sum(total, axis=0, keepdims=True)
        delta = jnp.sum(delta, axis=0, keepdims=True) * inverse
        for index, chunk in enumerate(chunks):
            attend = score_buf[chunk, :] * inverse
            score_grad = (attend * (weight_buf[chunk, :] - delta) * SCALE).astype(BF16)
            delta_buf[chunk, :] = score_grad
            key_terms = jnp.dot(score_grad, q_now, preferred_element_type=F32).astype(BF16)
            value_terms = jnp.dot(attend.astype(BF16), g_now, preferred_element_type=F32).astype(BF16)
            for part in range(per_chunk):
                s = index * per_chunk + part
                item = step * SELECTED + s
                stage[item, 0] = key_terms[part * BLOCK : (part + 1) * BLOCK]
                stage[item, 1] = value_terms[part * BLOCK : (part + 1) * BLOCK]
                store(step, s).start()
        query_terms = lax.dot_general(delta_buf[...], key_rows[...], rows_first, preferred_element_type=F32)
        grad_rows[span, :] = query_terms.astype(BF16)
        return carry

    lax.fori_loop(0, QBLOCKS, block, 0, unroll=True)
    for shift, result in enumerate(results):
        target = (plane + shift) % PLANES
        for owner in range(CORES):
            span = pl.ds(pl.multiple_of((target * CORES + owner) * PIECE, 16), PIECE)
            result[owner] = grad_rows[span, :]

    def finish(step, carry):
        for s in range(SELECTED):
            store(step, s).wait()
        return carry

    lax.fori_loop(0, QBLOCKS, finish, 0)


def attend_backward(slots, packed, fetched, parcels):
    rows = pltpu.VMEM((QBLOCKS * ROWS, HEAD_DIM), BF16)
    return pl.pallas_call(
        attend_kernel,
        out_shape=(array(CTX, 2, BLOCK, HEAD_DIM),) + (array(CORES, PIECE, HEAD_DIM),) * PLANES,
        in_specs=[IN_SMEM, IN_HBM, IN_VMEM] + [IN_VMEM] * PLANES,
        out_specs=(IN_HBM,) + (IN_VMEM,) * PLANES,
        scratch_shapes=[
            rows,
            rows,
            pltpu.VMEM((KEYS, HEAD_DIM), BF16),
            pltpu.VMEM((KEYS, HEAD_DIM), BF16),
            rows,
            pltpu.VMEM((KEYS, ROWS), F32),
            pltpu.VMEM((KEYS, ROWS), F32),
            pltpu.VMEM((KEYS, ROWS), BF16),
            pltpu.VMEM((QBLOCKS * SELECTED, 2, BLOCK, HEAD_DIM), BF16),
            pltpu.SemaphoreType.DMA((QBLOCKS * SELECTED,)),
        ],
        input_output_aliases={1: 0},
        compiler_params=pltpu.CompilerParams(vmem_limit_bytes=VMEM_ATTEND),
        name="attend_backward",
    )(slots, packed, fetched, *parcels)


def swap_kernel(*refs):
    parcels, (keep, send) = refs[:PLANES], refs[PLANES:]
    core = lax.axis_index("head") % CORES
    for shift, parcel in enumerate(parcels):
        keep[shift] = parcel[core]
        send[shift] = parcel[1 - core]


def swap(parcels):
    out = array(PLANES, PIECE, HEAD_DIM)
    return pl.pallas_call(
        swap_kernel,
        out_shape=(out, out),
        in_specs=[IN_VMEM] * PLANES,
        out_specs=(IN_VMEM, IN_VMEM),
        compiler_params=pltpu.CompilerParams(vmem_limit_bytes=VMEM_LIMIT),
        name="swap_cores",
    )(*parcels)


def merge_kernel(keep, got, query_grad):
    head = lax.axis_index("head")
    plane, core = head // CORES, head % CORES
    shape = (TOKENS // 2, 8, HEAD_DIM)
    even, odd = [], []
    for source in range(PLANES):
        shift = (plane - source + PLANES) % PLANES
        mine = keep[shift].astype(F32).reshape(shape)
        other = got[shift].astype(F32).reshape(shape)
        pair = halves(jnp.where(core == 0, mine, other), jnp.where(core == 0, other, mine))
        even.append(pair[0])
        odd.append(pair[1])
    both = jnp.stack([jnp.stack(even, 1), jnp.stack(odd, 1)], 1)
    query_grad[...] = both.reshape(TOKENS, PLANES * 8, HEAD_DIM).astype(BF16)


def merge(keep, got):
    return pl.pallas_call(
        merge_kernel,
        out_shape=array(TOKENS, PLANES * 8, HEAD_DIM),
        in_specs=[IN_VMEM, IN_VMEM],
        out_specs=IN_VMEM,
        compiler_params=pltpu.CompilerParams(vmem_limit_bytes=VMEM_LIMIT),
        name="merge_heads",
    )(keep, got)


def sum_kernel(rows, terms, key_grad, value_grad, sums, halves_out, sems):
    sums[...] = jnp.zeros_like(sums)

    def add(index, carry):
        row = wanted_row(rows, index)
        row = jnp.where(row < 0, OWNED, row)
        for kind in range(2):
            sums[kind, row] += terms[index, kind].astype(F32)
        return carry

    lax.fori_loop(0, CTX, add, 0, unroll=4)
    copies = []
    for kind, out in enumerate((key_grad, value_grad)):
        for part in range(2):
            span = pl.ds(part * (OWNED // 2), OWNED // 2)
            halves_out[kind, span] = sums[kind, span].astype(BF16)
            copies.append(pltpu.make_async_copy(halves_out.at[kind, span], out.at[span], sems.at[kind, part]))
            copies[-1].start()
    for copy in copies:
        copy.wait()


def owner_sum(rows, terms):
    grad = array(OWNED, BLOCK, HEAD_DIM)
    return pl.pallas_call(
        sum_kernel,
        out_shape=(grad, grad),
        in_specs=[IN_SMEM, IN_VMEM],
        out_specs=(IN_HBM, IN_HBM),
        scratch_shapes=[
            pltpu.VMEM((2, OWNED + 1, BLOCK, HEAD_DIM), F32),
            pltpu.VMEM((2, OWNED, BLOCK, HEAD_DIM), BF16),
            pltpu.SemaphoreType.DMA((2, 2)),
        ],
        compiler_params=pltpu.CompilerParams(vmem_limit_bytes=VMEM_LIMIT),
        name="owner_sum",
    )(rows, terms)


def exchange(blocks):
    return lax.all_to_all(blocks, "ctx", split_axis=0, concat_axis=0, tiled=True)


def swap_partner(array):
    return lax.ppermute(array, "head", [(i, i ^ 1) for i in range(PLANES * CORES)])


def along_planes(parcels):
    moved = [parcels[0]]
    for shift in range(1, PLANES):
        pairs = [(i, (i + shift * CORES) % (PLANES * CORES)) for i in range(PLANES * CORES)]
        moved.append(lax.ppermute(parcels[shift], "head", pairs))
    return moved


def per_device(queries, keys, values, out_grad, selected):
    ctx = lax.axis_index("ctx")
    table = selected[0].T
    slots = lax.dynamic_slice_in_dim(table, ctx * QBLOCKS, QBLOCKS, 1) // OWNED
    blocks = (OWNED, BLOCK, HEAD_DIM)
    packed, rows = pack(table, keys.reshape(blocks), values.reshape(blocks))
    fetched = exchange(packed)
    keep, send = split(rows, queries, out_grad)
    parcels = along_planes(join(keep, swap_partner(send)))
    terms, *results = attend_backward(slots, packed, fetched, parcels)
    back = exchange(terms)
    keep, send = swap(along_planes(results))
    query_grad = merge(keep, swap_partner(send))
    key_grad, value_grad = owner_sum(rows, back)
    return query_grad, key_grad.reshape(keys.shape), value_grad.reshape(values.shape)


def solution(mesh):
    tokens = P(("ctx", "head"), None, None)
    context = P("ctx", "head", None)
    return jax.shard_map(
        per_device,
        mesh=mesh,
        in_specs=(tokens, context, context, tokens, P("head", None, None)),
        out_specs=(tokens, context, context),
        check_vma=False,
    )
```

```python
import jax
import jax.numpy as jnp
from jax import lax
from jax.experimental import pallas as pl
from jax.experimental.pallas import tpu as pltpu
from jax.sharding import PartitionSpec as P

BLOCK = 64
SELECTED = 16
CTX = 64
OWNED = 32
QBLOCKS = 3
QBLOCKS_ALL = 192
HEAD_DIM = 128
GROUP_HEADS = 4
ROWS = BLOCK * GROUP_HEADS
KEYS = SELECTED * BLOCK
TOKENS = 12
PIECE = TOKENS * GROUP_HEADS
PLANES = 8
PAIRS = 4
CHUNK = 512
CORES = 2
SCALE = HEAD_DIM**-0.5
LOG2E = 1.4426950408889634
VMEM_LIMIT = 40 * 1024 * 1024
VMEM_ALL = 62 * 1024 * 1024
VMEM_ATTEND = 44 * 1024 * 1024
BF16 = jnp.bfloat16
F32 = jnp.float32
IN_VMEM = pl.BlockSpec(memory_space=pltpu.VMEM)
IN_SMEM = pl.BlockSpec(memory_space=pltpu.SMEM)
IN_HBM = pl.BlockSpec(memory_space=pltpu.HBM)


def array(*shape, dtype=BF16):
    return jax.ShapeDtypeStruct(shape, dtype)


def wanted_row(rows, index):
    first = rows[0, QBLOCKS * index]
    return jnp.maximum(jnp.maximum(first, rows[0, QBLOCKS * index + 1]), rows[0, QBLOCKS * index + 2])


def pack_kernel(table, keys, values, packed, rows, key_buf, value_buf, out_buf, table_buf, row_buf, in_sems, out_sems):
    picked = pltpu.make_async_copy(table, table_buf, in_sems.at[0])
    loads = [
        pltpu.make_async_copy(keys, key_buf, in_sems.at[1]),
        pltpu.make_async_copy(values, value_buf, in_sems.at[2]),
    ]
    picked.start()
    for load in loads:
        load.start()
    picked.wait()
    picks = table_buf[...]
    mine = jnp.where(picks // OWNED == lax.axis_index("ctx"), picks % OWNED, -1)
    row_buf[...] = jnp.max(mine, axis=0, keepdims=True)
    to_scalars = pltpu.make_async_copy(row_buf, rows, in_sems.at[3])
    to_scalars.start()
    to_scalars.wait()
    for load in loads:
        load.wait()
    parts = out_sems.shape[0]
    size = CTX // parts

    def store(part):
        span = pl.ds(part * size, size)
        return pltpu.make_async_copy(out_buf.at[span], packed.at[span], out_sems.at[part])

    for part in range(parts):

        def copy(index, carry):
            row = jnp.maximum(wanted_row(rows, index), 0)
            out_buf[index, 0] = key_buf[row]
            out_buf[index, 1] = value_buf[row]
            return carry

        lax.fori_loop(part * size, (part + 1) * size, copy, 0, unroll=4)
        store(part).start()
    for part in range(parts):
        store(part).wait()


def pack(table, keys, values):
    return pl.pallas_call(
        pack_kernel,
        out_shape=(array(CTX, 2, BLOCK, HEAD_DIM), array(1, QBLOCKS_ALL, dtype=jnp.int32)),
        in_specs=[IN_HBM, IN_HBM, IN_HBM],
        out_specs=(IN_HBM, IN_SMEM),
        scratch_shapes=[
            pltpu.VMEM((OWNED, BLOCK, HEAD_DIM), BF16),
            pltpu.VMEM((OWNED, BLOCK, HEAD_DIM), BF16),
            pltpu.VMEM((CTX, 2, BLOCK, HEAD_DIM), BF16),
            pltpu.VMEM((SELECTED, QBLOCKS_ALL), jnp.int32),
            pltpu.VMEM((1, QBLOCKS_ALL), jnp.int32),
            pltpu.SemaphoreType.DMA((4,)),
            pltpu.SemaphoreType.DMA((8,)),
        ],
        compiler_params=pltpu.CompilerParams(vmem_limit_bytes=VMEM_ALL),
        name="pack_blocks",
    )(table, keys, values)


def position():
    head = lax.axis_index("head")
    return head // (2 * CORES), head // CORES % 2, head % CORES


def plane_at(pair, low):
    return (pair + 2 * PAIRS) % PAIRS * 2 + low % 2


def halves(first, second):
    low = lax.broadcasted_iota(jnp.int32, first.shape, first.ndim - 2) < GROUP_HEADS
    axis = first.ndim - 2
    return (
        jnp.where(low, first, pltpu.roll(second, GROUP_HEADS, axis)),
        jnp.where(low, pltpu.roll(first, GROUP_HEADS, axis), second),
    )


def split_kernel(rows, queries, grads, keep, send):
    pair, low_bit, core = position()
    for kind, ref in enumerate((queries, grads)):
        tokens = ref[...].astype(F32).reshape(TOKENS // 2, 2, PLANES, 8, HEAD_DIM)
        low, high = halves(tokens[:, 0], tokens[:, 1])
        mine = jnp.where(core == 0, low, high).astype(BF16)
        other = jnp.where(core == 0, high, low).astype(BF16)
        for target in range(PLANES):
            shift = (target % 2 + low_bit) % 2 * PAIRS + (target // 2 - pair + PAIRS) % PAIRS
            keep[shift, kind] = mine[:, target].reshape(PIECE, HEAD_DIM)
            send[shift, kind] = other[:, target].reshape(PIECE, HEAD_DIM)


def split(rows, queries, grads):
    out = array(PLANES, 2, PIECE, HEAD_DIM)
    return pl.pallas_call(
        split_kernel,
        out_shape=(out, out),
        in_specs=[IN_SMEM, IN_VMEM, IN_VMEM],
        out_specs=(IN_VMEM, IN_VMEM),
        compiler_params=pltpu.CompilerParams(vmem_limit_bytes=VMEM_LIMIT),
        name="split_heads",
    )(rows, queries, grads)


def join_kernel(keep, got, near, far):
    for shift in range(PAIRS):
        near[shift, 0:2] = keep[shift]
        near[shift, 2:4] = got[shift]
        far[shift, 0:2] = keep[PAIRS + shift]
        far[shift, 2:4] = got[PAIRS + shift]


def link_kernel(near, far, *parcels):
    for shift, parcel in enumerate(parcels):
        parcel[0] = near[shift]
        parcel[1] = far[shift]


def part_kernel(*refs):
    parcels, (near, far) = refs[:PAIRS], refs[PAIRS:]
    for shift, parcel in enumerate(parcels):
        near[shift] = parcel[0]
        far[shift] = parcel[1]


def local(kernel, out_shape, name, *operands):
    return pl.pallas_call(
        kernel,
        out_shape=out_shape,
        in_specs=[IN_VMEM] * len(operands),
        out_specs=(IN_VMEM,) * len(out_shape),
        compiler_params=pltpu.CompilerParams(vmem_limit_bytes=VMEM_LIMIT),
        name=name,
    )(*operands)


def assemble_kernel(*refs):
    parcels, (q_rows, g_rows) = refs[:PAIRS], refs[PAIRS:]
    pair, low_bit, core = position()
    for shift, parcel in enumerate(parcels):
        for other in range(2):
            source = plane_at(pair - shift, low_bit + other)
            for piece, owner in ((0, core), (2, 1 - core)):
                span = pl.ds(pl.multiple_of((source * CORES + owner) * PIECE, 16), PIECE)
                q_rows[span, :] = parcel[other, piece]
                g_rows[span, :] = parcel[other, piece + 1]


def assemble(parcels):
    rows = array(QBLOCKS * ROWS, HEAD_DIM)
    return local(assemble_kernel, (rows, rows), "assemble_rows", *parcels)


def spread(grad_rows, results):
    pair, low_bit, core = position()
    for shift, result in enumerate(results):
        for other in range(2):
            target = plane_at(pair + shift, low_bit + other)
            for owner in range(CORES):
                span = pl.ds(pl.multiple_of((target * CORES + owner) * PIECE, 16), PIECE)
                result[other, owner] = grad_rows[span, :]


def attend_kernel(slots, unused, fetched, q_rows, g_rows, *refs):
    terms, results = refs[0], refs[1 : PAIRS + 1]
    all_keys, all_values, grad_rows, all_scores, all_weights, all_deltas, stage, sems = refs[PAIRS + 1 :]
    rows_first = (((0,), (0,)), ((), ()))
    chunks = [pl.ds(start, CHUNK) for start in range(0, KEYS, CHUNK)]
    per_chunk = CHUNK // BLOCK

    def fold(values, reduce):
        return reduce(values.reshape(CHUNK // 8, 8, ROWS), axis=0)

    def store(step, s):
        item = step * SELECTED + s
        return pltpu.make_async_copy(stage.at[item], terms.at[slots[s, step]], sems.at[item])

    def first(step):
        key_rows, value_rows = all_keys.at[step], all_values.at[step]
        score_buf, weight_buf, delta_buf = all_scores.at[step], all_weights.at[step], all_deltas.at[step]
        for s in range(SELECTED):
            slot = slots[s, step]
            key_rows[pl.ds(s * BLOCK, BLOCK), :] = fetched[slot, 0]
            value_rows[pl.ds(s * BLOCK, BLOCK), :] = fetched[slot, 1]
        span = pl.ds(step * ROWS, ROWS)
        q_now = q_rows[span, :]
        g_now = g_rows[span, :]
        q_flip, g_flip = q_now.T, g_now.T
        peak = jnp.full((8, ROWS), -jnp.inf, F32)
        for chunk in chunks:
            scores = jnp.dot(key_rows[chunk, :], q_flip, preferred_element_type=F32)
            score_buf[chunk, :] = scores
            peak = jnp.maximum(peak, fold(scores, jnp.max))
        peak = jnp.max(peak, axis=0, keepdims=True)
        return key_rows, value_rows, score_buf, weight_buf, delta_buf, span, q_now, g_now, g_flip, peak

    def second(step, state):
        key_rows, value_rows, score_buf, weight_buf, delta_buf, span, q_now, g_now, g_flip, peak = state
        total = jnp.zeros((8, ROWS), F32)
        delta = jnp.zeros((8, ROWS), F32)
        for chunk in chunks:
            weights = jnp.dot(value_rows[chunk, :], g_flip, preferred_element_type=F32)
            lifted = jnp.exp2((score_buf[chunk, :] - peak) * (SCALE * LOG2E))
            score_buf[chunk, :] = lifted
            weight_buf[chunk, :] = weights
            total += fold(lifted, jnp.sum)
            delta += fold(lifted * weights, jnp.sum)
        inverse = 1.0 / jnp.sum(total, axis=0, keepdims=True)
        delta = jnp.sum(delta, axis=0, keepdims=True) * inverse
        for index, chunk in enumerate(chunks):
            attend = score_buf[chunk, :] * inverse
            score_grad = (attend * (weight_buf[chunk, :] - delta) * SCALE).astype(BF16)
            delta_buf[chunk, :] = score_grad
            key_terms = jnp.dot(score_grad, q_now, preferred_element_type=F32).astype(BF16)
            value_terms = jnp.dot(attend.astype(BF16), g_now, preferred_element_type=F32).astype(BF16)
            for part in range(per_chunk):
                s = index * per_chunk + part
                item = step * SELECTED + s
                stage[item, 0] = key_terms[part * BLOCK : (part + 1) * BLOCK]
                stage[item, 1] = value_terms[part * BLOCK : (part + 1) * BLOCK]
                store(step, s).start()
        query_terms = lax.dot_general(delta_buf[...], key_rows[...], rows_first, preferred_element_type=F32)
        grad_rows[span, :] = query_terms.astype(BF16)

    states = [first(0)]
    for step in range(QBLOCKS):
        if step + 1 < QBLOCKS:
            states.append(first(step + 1))
        second(step, states[step])
    spread(grad_rows, results)

    def finish(step, carry):
        for s in range(SELECTED):
            store(step, s).wait()
        return carry

    lax.fori_loop(0, QBLOCKS, finish, 0)


def attend_backward(slots, packed, fetched, queries, grads):
    rows = pltpu.VMEM((QBLOCKS * ROWS, HEAD_DIM), BF16)
    return pl.pallas_call(
        attend_kernel,
        out_shape=(array(CTX, 2, BLOCK, HEAD_DIM),) + (array(2, CORES, PIECE, HEAD_DIM),) * PAIRS,
        in_specs=[IN_SMEM, IN_HBM, IN_VMEM, IN_VMEM, IN_VMEM],
        out_specs=(IN_HBM,) + (IN_VMEM,) * PAIRS,
        scratch_shapes=[
            pltpu.VMEM((QBLOCKS, KEYS, HEAD_DIM), BF16),
            pltpu.VMEM((QBLOCKS, KEYS, HEAD_DIM), BF16),
            rows,
            pltpu.VMEM((QBLOCKS, KEYS, ROWS), F32),
            pltpu.VMEM((QBLOCKS, KEYS, ROWS), F32),
            pltpu.VMEM((QBLOCKS, KEYS, ROWS), BF16),
            pltpu.VMEM((QBLOCKS * SELECTED, 2, BLOCK, HEAD_DIM), BF16),
            pltpu.SemaphoreType.DMA((QBLOCKS * SELECTED,)),
        ],
        input_output_aliases={1: 0},
        compiler_params=pltpu.CompilerParams(vmem_limit_bytes=VMEM_ATTEND),
        name="attend_backward",
    )(slots, packed, fetched, queries, grads)


def swap_kernel(near, far, keep, send):
    core = position()[2]
    for other, parcels in enumerate((near, far)):
        for shift in range(PAIRS):
            keep[other * PAIRS + shift] = parcels[shift, core]
            send[other * PAIRS + shift] = parcels[shift, 1 - core]


def merge_kernel(keep, got, query_grad):
    pair, low_bit, core = position()
    shape = (TOKENS // 2, 8, HEAD_DIM)
    even, odd = [], []
    for source in range(PLANES):
        shift = (source % 2 + low_bit) % 2 * PAIRS + (pair - source // 2 + PAIRS) % PAIRS
        mine = keep[shift].astype(F32).reshape(shape)
        other = got[shift].astype(F32).reshape(shape)
        joined = halves(jnp.where(core == 0, mine, other), jnp.where(core == 0, other, mine))
        even.append(joined[0])
        odd.append(joined[1])
    both = jnp.stack([jnp.stack(even, 1), jnp.stack(odd, 1)], 1)
    query_grad[...] = both.reshape(TOKENS, PLANES * 8, HEAD_DIM).astype(BF16)


def merge(keep, got):
    return pl.pallas_call(
        merge_kernel,
        out_shape=array(TOKENS, PLANES * 8, HEAD_DIM),
        in_specs=[IN_VMEM, IN_VMEM],
        out_specs=IN_VMEM,
        compiler_params=pltpu.CompilerParams(vmem_limit_bytes=VMEM_LIMIT),
        name="merge_heads",
    )(keep, got)


def sum_kernel(rows_in, terms, key_grad, value_grad, sums, halves_out, rows, sems, row_sem):
    fetch = pltpu.make_async_copy(rows_in, rows, row_sem)
    fetch.start()
    sums[...] = jnp.zeros_like(sums)
    fetch.wait()
    copies = []
    for kind, out in enumerate((key_grad, value_grad)):

        def add(index, carry):
            row = wanted_row(rows, index)
            row = jnp.where(row < 0, OWNED, row)
            sums[kind, row] += terms[index, kind].astype(F32)
            return carry

        lax.fori_loop(0, CTX, add, 0, unroll=8)
        for part in range(2):
            span = pl.ds(part * (OWNED // 2), OWNED // 2)
            halves_out[kind, span] = sums[kind, span].astype(BF16)
            copies.append(pltpu.make_async_copy(halves_out.at[kind, span], out.at[span], sems.at[kind, part]))
            copies[-1].start()
    for copy in copies:
        copy.wait()


def owner_sum(rows, terms):
    grad = array(OWNED, BLOCK, HEAD_DIM)
    return pl.pallas_call(
        sum_kernel,
        out_shape=(grad, grad),
        in_specs=[IN_HBM, IN_VMEM],
        out_specs=(IN_HBM, IN_HBM),
        scratch_shapes=[
            pltpu.VMEM((2, OWNED + 1, BLOCK, HEAD_DIM), F32),
            pltpu.VMEM((2, OWNED, BLOCK, HEAD_DIM), BF16),
            pltpu.SMEM((1, QBLOCKS_ALL), jnp.int32),
            pltpu.SemaphoreType.DMA((2, 2)),
            pltpu.SemaphoreType.DMA,
        ],
        compiler_params=pltpu.CompilerParams(vmem_limit_bytes=VMEM_LIMIT),
        name="owner_sum",
    )(rows, terms)


def exchange(blocks):
    return lax.all_to_all(blocks, "ctx", split_axis=0, concat_axis=0, tiled=True)


def swap_bit(block, bit):
    return lax.ppermute(block, "head", [(i, i ^ bit) for i in range(PLANES * CORES)])


def along_pairs(parcels):
    moved = [parcels[0]]
    for shift in range(1, PAIRS):
        pairs = [(i, (i + shift * 2 * CORES) % (PLANES * CORES)) for i in range(PLANES * CORES)]
        moved.append(lax.ppermute(parcels[shift], "head", pairs))
    return moved


def deliver(keep, send):
    half = array(PAIRS, 4, PIECE, HEAD_DIM)
    near, far = local(join_kernel, (half, half), "join_parcels", keep, swap_bit(send, 1))
    parcel = array(2, 4, PIECE, HEAD_DIM)
    return along_pairs(local(link_kernel, (parcel,) * PAIRS, "link_parcels", near, swap_bit(far, CORES)))


def send_back(results):
    half = array(PAIRS, CORES, PIECE, HEAD_DIM)
    near, far = local(part_kernel, (half, half), "part_parcels", *along_pairs(results))
    out = array(PLANES, PIECE, HEAD_DIM)
    keep, send = local(swap_kernel, (out, out), "swap_cores", near, swap_bit(far, CORES))
    return merge(keep, swap_bit(send, 1))


def per_device(queries, keys, values, out_grad, selected):
    ctx = lax.axis_index("ctx")
    table = selected[0].T
    slots = lax.dynamic_slice_in_dim(table, ctx * QBLOCKS, QBLOCKS, 1) // OWNED
    blocks = (OWNED, BLOCK, HEAD_DIM)
    packed, rows = pack(table, keys.reshape(blocks), values.reshape(blocks))
    fetched = exchange(packed)
    keep, send = split(rows, queries, out_grad)
    parcels = deliver(keep, send)
    terms, *results = attend_backward(slots, packed, fetched, *assemble(parcels))
    back = exchange(terms)
    query_grad = send_back(results)
    key_grad, value_grad = owner_sum(rows, back)
    return query_grad, key_grad.reshape(keys.shape), value_grad.reshape(values.shape)


def solution(mesh):
    tokens = P(("ctx", "head"), None, None)
    context = P("ctx", "head", None)
    return jax.shard_map(
        per_device,
        mesh=mesh,
        in_specs=(tokens, context, context, tokens, P("head", None, None)),
        out_specs=(tokens, context, context),
        check_vma=False,
    )
```
